32 devices in a mesh: tm: 4 (over y, x), space: 8 (over z, core).
Axes of the slice: x: 2, y: 2, z: 4, core: 2. Of those that a mesh axis runs over, the one named last changes fastest.
Arguments:
- guess: float32 [8, 256, 4096], P('tm', 'space'), may hold values from -6 to 6
- sources: bfloat16 [32, 256, 4096], P('tm', 'space'), may hold values from -6 to 6
- velocity: bfloat16 [4, 2, 256, 4096], P(None, None, 'space'), may hold values from -1 to 1
- snapshot: int32 [32], replicated, may hold values from 0 to 3
Outputs:
- c_values: float32 [8, 256, 4096], P('tm', 'space')
- control_grad: float32 [256, 4096], P('space', 'tm')
The draws below stay inside these ranges and needn't reach their ends.
Inputs may be any that keep to these rules, and one draw needn't show every extreme that they name: Each entry names a stored snapshot.
All inputs are finite; a program needn't handle non-finite values.
Results may differ from the reference program's by a relative error of at most 0.0003.
Values may be sent and summed in bfloat16 or wider, within the bound.
A program may use at most 128 MiB of HBM per device.

```python
import jax
import jax.numpy as jnp
from jax import lax

COLS = 4096
CF = 4
NSNAP = 4
NT = 32
NC = 8
NX = 256


def with_ends(values, key, low, top_value):
    longest = values.shape.index(max(values.shape))
    spots = []
    for shift in (0, 1):
        where = [jax.random.randint(jax.random.fold_in(key, axis), (), 0, length) for axis, length in enumerate(values.shape)]
        where[longest] = (where[longest] + shift) % values.shape[longest]
        spots.append(tuple(where))
    return values.at[spots[0]].set(low).at[spots[1]].set(top_value)


def levels(stream_key, dims, shards, least, top_value):
    factor_of, own = 1.0, jax.random.fold_in(stream_key, 6)
    for position, shards_of in shards:
        steps = jnp.exp(jax.random.uniform(jax.random.fold_in(own, position), (shards_of,), jnp.float32, least / len(shards), top_value / len(shards)))
        factor_of = factor_of * jnp.repeat(steps, dims[position] // shards_of).reshape([-1 if axis == position else 1 for axis in range(len(dims))])
    return factor_of


def noise(own_key, shape, width, most, split=(), kind=jnp.bfloat16):
    factor_of = levels(own_key, shape, split, -0.22, 0.18) if split else 1.0
    result = jax.random.normal(own_key, shape, jnp.float32) * width * factor_of
    return jnp.minimum(jnp.maximum(result, -most), most).astype(kind)


def setup_inputs(seed: int = 0) -> dict:
    key_list = jax.random.split(jax.random.key(seed), 5)
    guess = noise(key_list[0], (NC, NX, COLS), 1.0, 6.0, ((0, 4), (1, 8)), jnp.float32)
    sources = noise(key_list[1], (NT, NX, COLS), 1.0, 6.0, ((0, 4), (1, 8)))
    velocity = jnp.clip(jax.random.uniform(key_list[2], (NSNAP, 2, NX, COLS), jnp.float32, -1.0, 1.0) * levels(key_list[2], (NSNAP, 2, NX, COLS), ((2, 8),), -0.4, 0.0), -1.0, 1.0).astype(jnp.bfloat16)
    snapshot = with_ends(jax.random.randint(key_list[3], (NT,), 0, NSNAP), jax.random.fold_in(key_list[3], 1), 0, NSNAP - 1).astype(jnp.int32)
    return dict(guess=guess, sources=sources, velocity=velocity, snapshot=snapshot)


FINE_DIFF = 0.2
FINE_ADV = 0.3
COARSE_DIFF = 0.24
COARSE_ADV = 0.4


def shift_east(field):
    return jnp.concatenate([field[..., 1:], jnp.zeros_like(field[..., :1])], -1)


def shift_west(field):
    return jnp.concatenate([jnp.zeros_like(field[..., :1]), field[..., :-1]], -1)


def adjoint_step(state, speeds, diff, adv):
    speed_x = speeds[..., 0, :, :].astype(jnp.float32)
    speed_y = speeds[..., 1, :, :].astype(jnp.float32)
    centre = state[..., 1:-1, :]
    flux_x = speed_x * state
    flux_y = (speed_y * state)[..., 1:-1, :]
    laplace = state[..., 2:, :] + state[..., :-2, :] + shift_east(centre) + shift_west(centre) - 4.0 * centre
    advected = flux_x[..., 2:, :] - flux_x[..., :-2, :] + shift_east(flux_y) - shift_west(flux_y)
    return centre + diff * laplace + 0.5 * adv * advected


def pad_rows(field):
    widths = [(0, 0)] * (field.ndim - 2) + [(1, 1), (0, 0)]
    return jnp.pad(field, widths)


def reference(guess, sources, velocity, snapshot):
    def full_step(state, moment, diff, adv):
        speeds = lax.dynamic_index_in_dim(velocity, snapshot[moment], 0, keepdims=False)
        return adjoint_step(pad_rows(state), pad_rows(speeds), diff, adv)

    def relax(coarse_vals):
        tops = jnp.concatenate([coarse_vals[1:], jnp.zeros_like(coarse_vals[:1])], 0)

        def one_interval(items):
            state, interval = items
            time_total = jnp.zeros_like(state)
            for offset in range(CF - 1, 0, -1):
                moment = interval * CF + offset
                source = lax.dynamic_index_in_dim(sources, moment, 0, keepdims=False)
                state = full_step(state, moment, FINE_DIFF, FINE_ADV) + source.astype(jnp.float32)
                time_total = time_total + state
            return state, time_total

        return lax.map(one_interval, (tops, jnp.arange(NC, dtype=jnp.int32)))

    lowest, _ = relax(guess)

    def residual_of(items):
        state, interval, current = items
        moment = interval * CF
        source = lax.dynamic_index_in_dim(sources, moment, 0, keepdims=False)
        return full_step(state, moment, FINE_DIFF, FINE_ADV) + source.astype(jnp.float32) - current

    residual = lax.map(residual_of, (lowest, jnp.arange(NC, dtype=jnp.int32), guess))

    def coarse_fn(correction, items):
        res_term, interval = items
        correction = full_step(correction, interval * CF, COARSE_DIFF, COARSE_ADV) + res_term
        return correction, correction

    _, corr = lax.scan(coarse_fn, jnp.zeros_like(guess[0]), (residual, jnp.arange(NC, dtype=jnp.int32)), reverse=True)
    c_values = guess + corr
    _, f_totals = relax(c_values)
    control_grad = (jnp.sum(c_values, 0) + jnp.sum(f_totals, 0)) / NT
    return c_values, control_grad
```

```python
import functools

import jax
import jax.numpy as jnp
from jax import lax
from jax.experimental import pallas as pl
from jax.experimental.pallas import tpu as pltpu
from jax.sharding import PartitionSpec as P

FINE = (0.2, 0.15)
COARSE = (0.24, 0.2)
LANE = 128


def kernel(
    blocks,
    strips,
    snap_ref,
    guess_ref,
    src_ref,
    vel_ref,
    cval_ref,
    grad_ref,
    x_buf,
    next_guess,
    res_buf,
    b_buf,
    gathered,
    solved,
    incoming,
    corr_buf,
    total,
    totals_in,
    edge_out,
    edge_in,
    edge_send,
    edge_recv,
    big_send,
    big_recv,
):
    points, rows, cols = guess_ref.shape
    steps = src_ref.shape[0]
    factor = steps // points
    part = cols // blocks
    width = min(512, part)
    t = lax.axis_index("tm")
    s = lax.axis_index("space")
    has_up = s > 0
    has_down = s < strips - 1
    f32 = jnp.float32

    barrier = pltpu.get_barrier_semaphore()
    for d in range(1, blocks):
        pl.semaphore_signal(barrier, 1, device_id={"tm": lax.rem(t + d, blocks)})

    @pl.when(has_up)
    def _():
        pl.semaphore_signal(barrier, 1, device_id={"space": s - 1})

    @pl.when(has_down)
    def _():
        pl.semaphore_signal(barrier, 1, device_id={"space": s + 1})

    def clear_margin(ref, size):
        zero = jnp.zeros((rows, LANE), f32)
        ref[:, 0:LANE] = zero
        ref[:, size - LANE : size] = zero

    for c in range(points):
        for slot in range(2):
            clear_margin(x_buf.at[c, slot], cols + 2 * LANE)
        clear_margin(res_buf.at[c], cols + 2 * LANE)
        clear_margin(corr_buf.at[c], cols + 2 * LANE)
    clear_margin(next_guess, cols + 2 * LANE)
    clear_margin(b_buf, cols + 2 * LANE)
    clear_margin(incoming, cols + 2 * LANE)
    for i in range(blocks):
        clear_margin(gathered.at[i], part + 4 * LANE)
        for slot in range(2):
            clear_margin(solved.at[i, slot], part + 4 * LANE)
    rounds = edge_in.shape[0]

    @pl.when(jnp.logical_not(has_up))
    def _():
        def zero_top(i, carry):
            edge_in[i, 0] = jnp.zeros((1, cols), f32)
            return carry

        lax.fori_loop(0, rounds, zero_top, 0)

    @pl.when(jnp.logical_not(has_down))
    def _():
        def zero_bottom(i, carry):
            edge_in[i, 1] = jnp.zeros((1, cols), f32)
            return carry

        lax.fori_loop(0, rounds, zero_bottom, 0)

    def over_columns(fn):
        def step(k, carry):
            fn(pl.multiple_of(k * width, width))
            return carry

        lax.fori_loop(0, cols // width, step, 0)

    @pl.when(t == blocks - 1)
    def _():
        def clear(at):
            next_guess[:, pl.ds(at + LANE, width)] = jnp.zeros((rows, width), f32)
            incoming[:, pl.ds(at + LANE, width)] = jnp.zeros((rows, width), f32)

        over_columns(clear)

    peers = blocks - 1 + jnp.minimum(s, 1) + jnp.minimum(strips - 1 - s, 1)
    pl.semaphore_wait(barrier, peers)

    def edge_copies(idx, span):
        window = pl.ds(0, span)
        return (
            pltpu.make_async_remote_copy(
                edge_out.at[idx, 0, :, window],
                edge_in.at[idx, 1, :, window],
                edge_send.at[idx, 0],
                edge_recv.at[idx, 1],
                device_id={"space": s - 1},
            ),
            pltpu.make_async_remote_copy(
                edge_out.at[idx, 1, :, window],
                edge_in.at[idx, 0, :, window],
                edge_send.at[idx, 1],
                edge_recv.at[idx, 0],
                device_id={"space": s + 1},
            ),
        )

    used = []

    def send_edges(idx, span):
        used.append((idx, span))
        up, down = edge_copies(idx, span)

        @pl.when(has_up)
        def _():
            up.start()

        @pl.when(has_down)
        def _():
            down.start()

    def wait_edges(idx, span):
        up, down = edge_copies(idx, span)

        @pl.when(has_up)
        def _():
            down.wait_recv()

        @pl.when(has_down)
        def _():
            up.wait_recv()

    counter = [0]

    def new_edge():
        counter[0] += 1
        return counter[0] - 1

    def speed(snap, comp, at, size):
        return vel_ref[snap, comp, :, pl.ds(at, size)].astype(f32)

    row_no = lax.broadcasted_iota(jnp.int32, (rows, 1), 0)

    def stencil(src, at, vel_at, left_at, right_at, size, snap, kind, idx, edge_at):
        nu, h = kind
        p = src[:, pl.ds(at, size)]
        p_left = src[:, pl.ds(at - LANE, LANE)]
        p_right = src[:, pl.ds(at + size, LANE)]
        hay = h * speed(snap, 1, vel_at, size)
        hay_left = h * speed(snap, 1, left_at, LANE)
        hay_right = h * speed(snap, 1, right_at, LANE)
        hax = h * speed(snap, 0, vel_at, size)
        east = jnp.concatenate([(nu + hay) * p, (nu + hay_right) * p_right], 1)
        east = pltpu.roll(east, size + LANE - 1, 1)[:, :size]
        west = jnp.concatenate([(nu - hay_left) * p_left, (nu - hay) * p], 1)
        west = pltpu.roll(west, 1, 1)[:, LANE:]
        below = pltpu.roll((nu + hax) * p, rows - 1, 0)
        below = jnp.where(row_no == rows - 1, edge_in[idx, 1, :, pl.ds(edge_at, size)], below)
        above = pltpu.roll((nu - hax) * p, 1, 0)
        above = jnp.where(row_no == 0, edge_in[idx, 0, :, pl.ds(edge_at, size)], above)
        return (1.0 - 4.0 * nu) * p + (east + west) + (below + above)

    def put_edges(value, vel_at, size, snap, kind, idx, edge_at):
        nu, h = kind
        first = vel_ref[snap, 0, 0:16, pl.ds(vel_at, size)].astype(f32)[0:1]
        last = vel_ref[snap, 0, rows - 16 : rows, pl.ds(vel_at, size)].astype(f32)[15:16]
        edge_out[idx, 0, :, pl.ds(edge_at, size)] = (nu + h * first) * value[0:1]
        edge_out[idx, 1, :, pl.ds(edge_at, size)] = (nu - h * last) * value[rows - 1 : rows]

    def snap_at(local):
        return snap_ref[t * steps + local]

    def full_stencil(src, at, snap, kind, idx):
        left = pl.multiple_of(jnp.maximum(at - LANE, 0), LANE)
        right = pl.multiple_of(jnp.minimum(at + width, cols - LANE), LANE)
        return stencil(src, at + LANE, at, left, right, width, snap, kind, idx, at)

    def guess_copy():
        return pltpu.make_async_remote_copy(
            guess_ref.at[0],
            next_guess.at[:, pl.ds(LANE, cols)],
            big_send.at[0, 0],
            big_recv.at[0, 0],
            device_id={"tm": t - 1},
        )

    @pl.when(t > 0)
    def _():
        guess_copy().start()

    def relax_chain(c, make_src, finish_last, with_residual, accumulate):
        src = make_src()
        idx = new_edge()
        snap = snap_at(c * factor + factor - 1)

        def first(at):
            put_edges(src[:, pl.ds(at + LANE, width)], at, width, snap, FINE, idx, at)

        over_columns(first)
        send_edges(idx, cols)
        yield
        slot = 1
        last = 0 if with_residual else 1
        for offset in range(factor - 1, last - 1, -1):
            n = c * factor + offset
            snap = snap_at(n)
            dst = x_buf.at[c, slot]
            more = offset > last
            nxt = new_edge() if more else None
            snap_next = snap_at(n - 1) if more else None
            wait_edges(idx, cols)

            def work(at, src=src, dst=dst, idx=idx, nxt=nxt, snap=snap, snap_next=snap_next, n=n, offset=offset, more=more):
                new = full_stencil(src, at, snap, FINE, idx)
                new = new + src_ref[n, :, pl.ds(at, width)].astype(f32)
                if more:
                    put_edges(new, at, width, snap_next, FINE, nxt, at)
                    dst[:, pl.ds(at + LANE, width)] = new
                if accumulate:
                    total[:, pl.ds(at, width)] += new
                if offset == 0:
                    finish_last(at, new)

            over_columns(work)
            if more:
                send_edges(nxt, cols)
            src, idx, slot = dst, nxt, 1 - slot
            yield

    def run(chains):
        chains = list(chains)
        while chains:
            alive = []
            for chain in chains:
                try:
                    next(chain)
                    alive.append(chain)
                except StopIteration:
                    pass
            chains = alive

    first_coarse = new_edge()
    snap_coarse = [snap_at(c * factor) for c in range(points)]

    def first_src(c):
        def make():
            if c < points - 1:

                def fill(at):
                    x_buf[c, 0, :, pl.ds(at + LANE, width)] = guess_ref[c + 1, :, pl.ds(at, width)]

                over_columns(fill)
                return x_buf.at[c, 0]

            @pl.when(t < blocks - 1)
            def _():
                guess_copy().wait_recv()

            return next_guess

        return make

    def first_last(c):
        def finish(at, new):
            value = new - guess_ref[c, :, pl.ds(at, width)]
            res_buf[c, :, pl.ds(at + LANE, width)] = value
            if c == points - 1 and points > 1:
                put_edges(value, at, width, snap_coarse[points - 2], COARSE, first_coarse, at)
            if points == 1:
                b_buf[:, pl.ds(at + LANE, width)] = value

        return finish

    for c in range(points - 1):
        run([relax_chain(c, first_src(c), first_last(c), True, False)])
    run([relax_chain(points - 1, first_src(points - 1), first_last(points - 1), True, False)])

    src, idx = res_buf.at[points - 1], first_coarse
    if points > 1:
        send_edges(idx, cols)
    for i in range(points - 2, -1, -1):
        nxt = new_edge() if i > 0 else None
        dst = b_buf if i == 0 else x_buf.at[0, i % 2]
        wait_edges(idx, cols)

        def condense(at, src=src, dst=dst, idx=idx, nxt=nxt, i=i):
            new = full_stencil(src, at, snap_coarse[i], COARSE, idx)
            new = new + res_buf[i, :, pl.ds(at + LANE, width)]
            dst[:, pl.ds(at + LANE, width)] = new
            if i > 0:
                put_edges(new, at, width, snap_coarse[i - 1], COARSE, nxt, at)

        over_columns(condense)
        if i > 0:
            send_edges(nxt, cols)
        src, idx = dst, nxt

    wide = part + 2 * LANE

    def slab_copy(to, sender):
        return pltpu.make_async_remote_copy(
            b_buf.at[:, pl.ds(pl.multiple_of(to * part, LANE), wide)],
            gathered.at[sender, :, pl.ds(LANE, wide)],
            big_send.at[1, to],
            big_recv.at[1, sender],
            device_id={"tm": to},
        )

    @pl.when(t > 0)
    def _():
        for to in range(blocks):

            @pl.when(t != to)
            def _():
                slab_copy(to, t).start()

        for at in range(0, wide, LANE):
            gathered[t, :, at + LANE : at + 2 * LANE] = b_buf[
                :, pl.ds(pl.multiple_of(t * part + at, LANE), LANE)
            ]

    def incoming_copy(block, ref, sender):
        return pltpu.make_async_remote_copy(
            ref.at[:, pl.ds(2 * LANE, part)],
            incoming.at[:, pl.ds(pl.multiple_of(LANE + sender * part, LANE), part)],
            big_send.at[2, block],
            big_recv.at[2, sender],
            device_id={"tm": block},
        )

    pieces = [(0, LANE)]
    pieces += [(LANE + k * width, width) for k in range(part // width)]
    pieces += [(LANE + part, LANE)]
    base = t * part - LANE

    def clip(at):
        return pl.multiple_of(jnp.clip(base + at, 0, cols - LANE), LANE)

    def piece_vel(at, size):
        if size == LANE:
            return clip(at)
        return pl.multiple_of(base + at, LANE)

    def need(block):
        @pl.when(t != block)
        def _():
            slab_copy(t, block).wait_recv()

    def deliver(block, ref):
        @pl.when(t != block)
        def _():
            incoming_copy(block, ref, t).start()

        @pl.when(t == block)
        def _():
            for at in range(0, part, LANE):
                incoming[:, pl.ds(pl.multiple_of(LANE + t * part + at, LANE), LANE)] = ref[
                    :, 2 * LANE + at : 3 * LANE + at
                ]

    need(blocks - 1)
    src = gathered.at[blocks - 1]
    delivered = []
    if blocks > 1:
        deliver(blocks - 2, src)
        delivered.append((blocks - 2, src))
    chain = [(block, i) for block in range(blocks - 2, 0, -1) for i in range(points - 1, -1, -1)]

    def part_snap(block, i):
        return snap_ref[(block * points + i) * factor]

    if chain:
        idx = new_edge()
        for at, size in pieces:
            put_edges(src[:, at + LANE : at + LANE + size], piece_vel(at, size), size, part_snap(*chain[0]), COARSE, idx, at)
        send_edges(idx, wide)
    for number, (block, i) in enumerate(chain):
        more = number + 1 < len(chain)
        nxt = new_edge() if more else None
        dst = solved.at[block, i % 2]
        if i == 0:
            need(block)
        wait_edges(idx, wide)
        for at, size in pieces:
            new = stencil(
                src, at + LANE, piece_vel(at, size), clip(at - LANE), clip(at + size), size,
                part_snap(block, i), COARSE, idx, at,
            )
            if i == 0:
                new = new + gathered[block, :, at + LANE : at + LANE + size]
            if at == 0:
                new = jnp.where(t > 0, new, 0.0)
            if at == LANE + part:
                new = jnp.where(t < blocks - 1, new, 0.0)
            dst[:, at + LANE : at + LANE + size] = new
            if more:
                put_edges(new, piece_vel(at, size), size, part_snap(*chain[number + 1]), COARSE, nxt, at)
        if more:
            send_edges(nxt, wide)
        if i == 0:
            deliver(block - 1, dst)
            delivered.append((block - 1, dst))
        src, idx = dst, nxt

    for sender in range(blocks):

        @pl.when(jnp.logical_and(t < blocks - 1, t != sender))
        def _():
            incoming_copy(t, gathered.at[0], sender).wait_recv()

    ready = set()
    idx_corr = new_edge()

    def start_all(at):
        value = incoming[:, pl.ds(at + LANE, width)]
        put_edges(value, at, width, snap_coarse[points - 1], COARSE, idx_corr, at)
        x_buf[points - 1, 0, :, pl.ds(at + LANE, width)] = value + next_guess[:, pl.ds(at + LANE, width)]
        total[:, pl.ds(at, width)] = jnp.zeros((rows, width), f32)

    over_columns(start_all)
    send_edges(idx_corr, cols)

    def correction_chain():
        src, idx = incoming, idx_corr
        for i in range(points - 1, -1, -1):
            nxt = new_edge() if i > 0 else None
            dst = corr_buf.at[i]
            wait_edges(idx, cols)

            def work(at, src=src, dst=dst, idx=idx, nxt=nxt, i=i):
                new = full_stencil(src, at, snap_coarse[i], COARSE, idx)
                new = new + res_buf[i, :, pl.ds(at + LANE, width)]
                value = guess_ref[i, :, pl.ds(at, width)] + new
                cval_ref[i, :, pl.ds(at, width)] = value
                total[:, pl.ds(at, width)] += value
                if i > 0:
                    dst[:, pl.ds(at + LANE, width)] = new
                    put_edges(new, at, width, snap_coarse[i - 1], COARSE, nxt, at)
                    x_buf[i - 1, 0, :, pl.ds(at + LANE, width)] = value

            over_columns(work)
            if i > 0:
                send_edges(nxt, cols)
                ready.add(i - 1)
            src, idx = dst, nxt
            yield

    def second_chain(c):
        while c < points - 1 and c not in ready:
            yield
        yield from relax_chain(c, lambda: x_buf.at[c, 0], None, False, True)

    run([second_chain(points - 1), correction_chain()] + [second_chain(c) for c in range(points - 2, -1, -1)])

    def total_copy(to, sender):
        return pltpu.make_async_remote_copy(
            total.at[:, pl.ds(pl.multiple_of(to * part, LANE), part)],
            totals_in.at[sender],
            big_send.at[3, to],
            big_recv.at[3, sender],
            device_id={"tm": to},
        )

    for to in range(blocks):

        @pl.when(t != to)
        def _():
            total_copy(to, t).start()

    for idx, span in used:
        up, down = edge_copies(idx, span)

        @pl.when(has_up)
        def _():
            up.wait_send()

        @pl.when(has_down)
        def _():
            down.wait_send()

    @pl.when(t > 0)
    def _():
        guess_copy().wait_send()
        for to in range(blocks):

            @pl.when(t != to)
            def _():
                slab_copy(to, t).wait_send()

    for block, ref in delivered:

        @pl.when(t != block)
        def _():
            incoming_copy(block, ref, t).wait_send()

    for other in range(blocks):

        @pl.when(t != other)
        def _():
            total_copy(t, other).wait_recv()

    scale = 1.0 / (steps * blocks)
    for at in range(0, part, width):
        own = total[:, pl.ds(pl.multiple_of(t * part + at, LANE), width)]
        for other in range(blocks):
            got = totals_in[other, :, at : at + width]
            own = own + jnp.where(t == other, 0.0, got)
        grad_ref[:, at : at + width] = own * scale
    for to in range(blocks):

        @pl.when(t != to)
        def _():
            total_copy(to, t).wait_send()


def body(blocks, strips, guess, sources, velocity, snapshot):
    points, rows, cols = guess.shape
    steps = sources.shape[0]
    factor = steps // points
    part = cols // blocks
    padded = cols + 2 * LANE
    edges = points * (2 * factor + 1) + 2 * points + points * blocks
    f32 = jnp.float32
    vmem = pl.BlockSpec(memory_space=pltpu.VMEM)
    return pl.pallas_call(
        functools.partial(kernel, blocks, strips),
        out_shape=(
            jax.ShapeDtypeStruct((points, rows, cols), f32),
            jax.ShapeDtypeStruct((rows, part), f32),
        ),
        in_specs=[pl.BlockSpec(memory_space=pltpu.SMEM), vmem, vmem, vmem],
        out_specs=(vmem, vmem),
        scratch_shapes=[
            pltpu.VMEM((points, 2, rows, padded), f32),
            pltpu.VMEM((rows, padded), f32),
            pltpu.VMEM((points, rows, padded), f32),
            pltpu.VMEM((rows, padded), f32),
            pltpu.VMEM((blocks, rows, part + 4 * LANE), f32),
            pltpu.VMEM((blocks, 2, rows, part + 4 * LANE), f32),
            pltpu.VMEM((rows, padded), f32),
            pltpu.VMEM((points, rows, padded), f32),
            pltpu.VMEM((rows, cols), f32),
            pltpu.VMEM((blocks, rows, part), f32),
            pltpu.VMEM((edges, 2, 1, cols), f32),
            pltpu.VMEM((edges, 2, 1, cols), f32),
            pltpu.SemaphoreType.DMA((edges, 2)),
            pltpu.SemaphoreType.DMA((edges, 2)),
            pltpu.SemaphoreType.DMA((4, blocks)),
            pltpu.SemaphoreType.DMA((4, blocks)),
        ],
        compiler_params=pltpu.CompilerParams(
            collective_id=0, has_side_effects=True, vmem_limit_bytes=56 * 1024 * 1024
        ),
    )(snapshot, guess, sources, velocity)


def solution(mesh):
    in_specs = (P("tm", "space", None), P("tm", "space", None), P(None, None, "space", None), P())
    out_specs = (P("tm", "space", None), P("space", "tm"))
    fn = functools.partial(body, mesh.shape["tm"], mesh.shape["space"])
    return jax.shard_map(fn, mesh=mesh, in_specs=in_specs, out_specs=out_specs, check_vma=False)
```

```python
import functools

import jax
import jax.numpy as jnp
from jax import lax
from jax.experimental import pallas as pl
from jax.experimental.pallas import tpu as pltpu
from jax.sharding import PartitionSpec as P

FINE = (0.2, 0.15)
COARSE = (0.24, 0.2)
LANE = 128


def kernel(
    blocks,
    strips,
    snap_ref,
    guess_ref,
    src_ref,
    vel_ref,
    cval_ref,
    grad_ref,
    x_buf,
    next_guess,
    res_buf,
    b_buf,
    gathered,
    solved,
    incoming,
    corr_buf,
    total,
    totals_in,
    edge_out,
    edge_in,
    edge_send,
    edge_recv,
    side_speed,
    side_send,
    side_recv,
    big_send,
    big_recv,
):
    points, rows, cols = guess_ref.shape
    steps = src_ref.shape[0]
    factor = steps // points
    part = cols // blocks
    width = min(1024, part)
    deep = (gathered.shape[1] - rows) // 2
    wide = part + 2 * LANE
    t = lax.axis_index("tm")
    s = lax.axis_index("space")
    has_up = s > 0
    has_down = s < strips - 1
    f32 = jnp.float32

    barrier = pltpu.get_barrier_semaphore()
    for d in range(1, blocks):
        pl.semaphore_signal(barrier, 1, device_id={"tm": lax.rem(t + d, blocks)})

    @pl.when(has_up)
    def _():
        pl.semaphore_signal(barrier, 1, device_id={"space": s - 1})

    @pl.when(has_down)
    def _():
        pl.semaphore_signal(barrier, 1, device_id={"space": s + 1})

    def clear_margin(ref, size):
        zero = jnp.zeros((ref.shape[0], LANE), f32)
        ref[:, 0:LANE] = zero
        ref[:, size - LANE : size] = zero

    for c in range(points):
        for slot in range(2):
            clear_margin(x_buf.at[c, slot], cols + 2 * LANE)
        clear_margin(res_buf.at[c], cols + 2 * LANE)
        clear_margin(corr_buf.at[c], cols + 2 * LANE)
    clear_margin(next_guess, cols + 2 * LANE)
    clear_margin(b_buf, cols + 2 * LANE)
    clear_margin(incoming, cols + 2 * LANE)
    for i in range(blocks):
        clear_margin(gathered.at[i], part + 4 * LANE)
        for slot in range(2):
            clear_margin(solved.at[i, slot], part + 4 * LANE)
    rounds = edge_in.shape[0]

    @pl.when(jnp.logical_not(has_up))
    def _():
        def zero_top(i, carry):
            edge_in[i, 0] = jnp.zeros((1, cols), f32)
            return carry

        lax.fori_loop(0, rounds, zero_top, 0)
        side_speed[0] = jnp.zeros(side_speed.shape[1:], side_speed.dtype)
        for block in range(2, blocks):
            gathered[block, 0:deep, LANE : LANE + wide] = jnp.zeros((deep, wide), f32)

    @pl.when(jnp.logical_not(has_down))
    def _():
        def zero_bottom(i, carry):
            edge_in[i, 1] = jnp.zeros((1, cols), f32)
            return carry

        lax.fori_loop(0, rounds, zero_bottom, 0)
        side_speed[1] = jnp.zeros(side_speed.shape[1:], side_speed.dtype)
        for block in range(2, blocks):
            gathered[block, deep + rows : rows + 2 * deep, LANE : LANE + wide] = jnp.zeros((deep, wide), f32)

    def over_columns(fn):
        def step(k, carry):
            fn(pl.multiple_of(k * width, width))
            return carry

        lax.fori_loop(0, cols // width, step, 0)

    @pl.when(t == blocks - 1)
    def _():
        def clear(at):
            next_guess[:, pl.ds(at + LANE, width)] = jnp.zeros((rows, width), f32)
            incoming[:, pl.ds(at + LANE, width)] = jnp.zeros((rows, width), f32)

        over_columns(clear)

    peers = blocks - 1 + jnp.minimum(s, 1) + jnp.minimum(strips - 1 - s, 1)
    pl.semaphore_wait(barrier, peers)

    def edge_copies(idx, span):
        window = pl.ds(0, span)
        return (
            pltpu.make_async_remote_copy(
                edge_out.at[idx, 0, :, window],
                edge_in.at[idx, 1, :, window],
                edge_send.at[idx, 0],
                edge_recv.at[idx, 1],
                device_id={"space": s - 1},
            ),
            pltpu.make_async_remote_copy(
                edge_out.at[idx, 1, :, window],
                edge_in.at[idx, 0, :, window],
                edge_send.at[idx, 1],
                edge_recv.at[idx, 0],
                device_id={"space": s + 1},
            ),
        )

    used = []

    def send_edges(idx, span):
        used.append((idx, span))
        up, down = edge_copies(idx, span)

        @pl.when(has_up)
        def _():
            up.start()

        @pl.when(has_down)
        def _():
            down.start()

    def wait_edges(idx, span):
        up, down = edge_copies(idx, span)

        @pl.when(has_up)
        def _():
            down.wait_recv()

        @pl.when(has_down)
        def _():
            up.wait_recv()

    counter = [0]

    def new_edge():
        counter[0] += 1
        return counter[0] - 1

    def speed(snap, comp, at, size):
        return vel_ref[snap, comp, :, pl.ds(at, size)].astype(f32)

    row_no = lax.broadcasted_iota(jnp.int32, (rows, 1), 0)

    def stencil(src, at, vel_at, left_at, right_at, size, snap, kind, idx, edge_at, speed_of=None):
        nu, h = kind
        speed_of = speed_of or speed
        p = src[:, pl.ds(at, size)]
        p_left = src[:, pl.ds(at - LANE, LANE)]
        p_right = src[:, pl.ds(at + size, LANE)]
        hay = h * speed_of(snap, 1, vel_at, size)
        hay_left = h * speed_of(snap, 1, left_at, LANE)
        hay_right = h * speed_of(snap, 1, right_at, LANE)
        hax = h * speed_of(snap, 0, vel_at, size)
        east = jnp.concatenate([(nu + hay) * p, (nu + hay_right) * p_right], 1)
        east = pltpu.roll(east, size + LANE - 1, 1)[:, :size]
        west = jnp.concatenate([(nu - hay_left) * p_left, (nu - hay) * p], 1)
        west = pltpu.roll(west, 1, 1)[:, LANE:]
        below = pltpu.roll((nu + hax) * p, p.shape[0] - 1, 0)
        above = pltpu.roll((nu - hax) * p, 1, 0)
        if idx is not None:
            below = jnp.where(row_no == rows - 1, edge_in[idx, 1, :, pl.ds(edge_at, size)], below)
            above = jnp.where(row_no == 0, edge_in[idx, 0, :, pl.ds(edge_at, size)], above)
        return (1.0 - 4.0 * nu) * p + (east + west) + (below + above)

    def put_edges(value, vel_at, size, snap, kind, idx, edge_at):
        nu, h = kind
        first = vel_ref[snap, 0, 0:16, pl.ds(vel_at, size)].astype(f32)[0:1]
        last = vel_ref[snap, 0, rows - 16 : rows, pl.ds(vel_at, size)].astype(f32)[15:16]
        edge_out[idx, 0, :, pl.ds(edge_at, size)] = (nu + h * first) * value[0:1]
        edge_out[idx, 1, :, pl.ds(edge_at, size)] = (nu - h * last) * value[rows - 1 : rows]

    def snap_at(local):
        return snap_ref[t * steps + local]

    def full_stencil(src, at, snap, kind, idx):
        left = pl.multiple_of(jnp.maximum(at - LANE, 0), LANE)
        right = pl.multiple_of(jnp.minimum(at + width, cols - LANE), LANE)
        return stencil(src, at + LANE, at, left, right, width, snap, kind, idx, at)

    def guess_copy():
        return pltpu.make_async_remote_copy(
            guess_ref.at[0],
            next_guess.at[:, pl.ds(LANE, cols)],
            big_send.at[0, 0],
            big_recv.at[0, 0],
            device_id={"tm": t - 1},
        )

    @pl.when(t > 0)
    def _():
        guess_copy().start()

    vel_start = pl.multiple_of(jnp.clip(t * part - LANE, 0, cols - wide), LANE)

    def to_sides(up_src, up_dst, down_src, down_dst, number):
        return (
            pltpu.make_async_remote_copy(
                up_src, up_dst, side_send.at[number, 0], side_recv.at[number, 1], device_id={"space": s - 1}
            ),
            pltpu.make_async_remote_copy(
                down_src, down_dst, side_send.at[number, 1], side_recv.at[number, 0], device_id={"space": s + 1}
            ),
        )

    def speed_sides():
        window = pl.ds(vel_start, wide)
        return to_sides(
            vel_ref.at[:, :, 0:16, window],
            side_speed.at[1],
            vel_ref.at[:, :, rows - 16 : rows, window],
            side_speed.at[0],
            0,
        )

    def slab_sides(block):
        window = pl.ds(LANE, wide)
        return to_sides(
            gathered.at[block, deep : 2 * deep, window],
            gathered.at[block, deep + rows : rows + 2 * deep, window],
            gathered.at[block, rows : rows + deep, window],
            gathered.at[block, 0:deep, window],
            block,
        )

    def start_sides(copies):
        up, down = copies

        @pl.when(has_up)
        def _():
            up.start()

        @pl.when(has_down)
        def _():
            down.start()

    def wait_sides(copies):
        up, down = copies

        @pl.when(has_up)
        def _():
            down.wait_recv()

        @pl.when(has_down)
        def _():
            up.wait_recv()

    def sent_sides(copies):
        up, down = copies

        @pl.when(has_up)
        def _():
            up.wait_send()

        @pl.when(has_down)
        def _():
            down.wait_send()

    def relax_chain(c, make_src, finish_last, with_residual, accumulate):
        src = make_src()
        idx = new_edge()
        snap = snap_at(c * factor + factor - 1)

        def first(at):
            put_edges(src[:, pl.ds(at + LANE, width)], at, width, snap, FINE, idx, at)

        over_columns(first)
        send_edges(idx, cols)
        yield
        slot = 1
        last = 0 if with_residual else 1
        for offset in range(factor - 1, last - 1, -1):
            n = c * factor + offset
            snap = snap_at(n)
            dst = x_buf.at[c, slot]
            more = offset > last
            nxt = new_edge() if more else None
            snap_next = snap_at(n - 1) if more else None
            wait_edges(idx, cols)

            def work(at, src=src, dst=dst, idx=idx, nxt=nxt, snap=snap, snap_next=snap_next, n=n, offset=offset, more=more):
                new = full_stencil(src, at, snap, FINE, idx)
                new = new + src_ref[n, :, pl.ds(at, width)].astype(f32)
                if more:
                    put_edges(new, at, width, snap_next, FINE, nxt, at)
                    dst[:, pl.ds(at + LANE, width)] = new
                if accumulate:
                    total[:, pl.ds(at, width)] += new
                if offset == 0:
                    finish_last(at, new)

            over_columns(work)
            if more:
                send_edges(nxt, cols)
            src, idx, slot = dst, nxt, 1 - slot
            yield

    lead = 2

    def run(chains):
        chains = list(chains)
        while chains:
            alive = []
            for chain in chains:
                try:
                    next(chain)
                    alive.append(chain)
                except StopIteration:
                    pass
            chains = alive

    first_coarse = new_edge()
    snap_coarse = [snap_at(c * factor) for c in range(points)]

    def first_src(c):
        def make():
            if c < points - 1:

                def fill(at):
                    x_buf[c, 0, :, pl.ds(at + LANE, width)] = guess_ref[c + 1, :, pl.ds(at, width)]

                over_columns(fill)
                return x_buf.at[c, 0]

            @pl.when(t < blocks - 1)
            def _():
                guess_copy().wait_recv()

            return next_guess

        return make

    def first_last(c):
        def finish(at, new):
            value = new - guess_ref[c, :, pl.ds(at, width)]
            res_buf[c, :, pl.ds(at + LANE, width)] = value
            if c == points - 1 and points > 1:
                put_edges(value, at, width, snap_coarse[points - 2], COARSE, first_coarse, at)
            if points == 1:
                b_buf[:, pl.ds(at + LANE, width)] = value

        return finish

    chains = [relax_chain(c, first_src(c), first_last(c), True, False) for c in range(points)]
    for c in range(points - 1):
        for _ in range(lead):
            next(chains[c], None)
    start_sides(speed_sides())
    run(chains)

    src, idx = res_buf.at[points - 1], first_coarse
    if points > 1:
        send_edges(idx, cols)
    for i in range(points - 2, -1, -1):
        nxt = new_edge() if i > 0 else None
        dst = b_buf if i == 0 else x_buf.at[0, i % 2]
        wait_edges(idx, cols)

        def condense(at, src=src, dst=dst, idx=idx, nxt=nxt, i=i):
            new = full_stencil(src, at, snap_coarse[i], COARSE, idx)
            new = new + res_buf[i, :, pl.ds(at + LANE, width)]
            dst[:, pl.ds(at + LANE, width)] = new
            if i > 0:
                put_edges(new, at, width, snap_coarse[i - 1], COARSE, nxt, at)

        over_columns(condense)
        if i > 0:
            send_edges(nxt, cols)
        src, idx = dst, nxt

    def slab_copy(to, sender):
        return pltpu.make_async_remote_copy(
            b_buf.at[:, pl.ds(pl.multiple_of(to * part, LANE), wide)],
            gathered.at[sender, deep : deep + rows, pl.ds(LANE, wide)],
            big_send.at[1, to],
            big_recv.at[1, sender],
            device_id={"tm": to},
        )

    @pl.when(t > 0)
    def _():
        for to in range(blocks):

            @pl.when(t != to)
            def _():
                slab_copy(to, t).start()

        for at in range(0, wide, LANE):
            gathered[t, deep : deep + rows, at + LANE : at + 2 * LANE] = b_buf[
                :, pl.ds(pl.multiple_of(t * part + at, LANE), LANE)
            ]

    def incoming_copy(block, ref, sender):
        return pltpu.make_async_remote_copy(
            ref.at[deep : deep + rows, pl.ds(2 * LANE, part)],
            incoming.at[:, pl.ds(pl.multiple_of(LANE + sender * part, LANE), part)],
            big_send.at[2, block],
            big_recv.at[2, sender],
            device_id={"tm": block},
        )

    piece = min(512, part)
    pieces = [(0, LANE)]
    pieces += [(LANE + k * piece, piece) for k in range(part // piece)]
    pieces += [(LANE + part, LANE)]
    base = t * part - LANE

    def clip(at):
        return pl.multiple_of(jnp.clip(base + at, 0, cols - LANE), LANE)

    def piece_vel(at, size):
        if size == LANE:
            return clip(at)
        return pl.multiple_of(base + at, LANE)

    def need(block):
        @pl.when(t != block)
        def _():
            slab_copy(t, block).wait_recv()

    def deliver(block, ref):
        @pl.when(t != block)
        def _():
            incoming_copy(block, ref, t).start()

        @pl.when(t == block)
        def _():
            for at in range(0, part, LANE):
                incoming[:, pl.ds(pl.multiple_of(LANE + t * part + at, LANE), LANE)] = ref[
                    deep : deep + rows, 2 * LANE + at : 3 * LANE + at
                ]

    need(blocks - 1)
    src = gathered.at[blocks - 1]
    delivered = []
    if blocks > 1:
        deliver(blocks - 2, src)
        delivered.append((blocks - 2, src))
    chain = [(block, i) for block in range(blocks - 2, 0, -1) for i in range(points - 1, -1, -1)]

    def part_snap(block, i):
        return snap_ref[(block * points + i) * factor]

    all_rows = lax.broadcasted_iota(jnp.int32, (rows + 2 * deep, 1), 0)
    inside = jnp.logical_or(all_rows >= deep, has_up)
    inside = jnp.logical_and(inside, jnp.logical_or(all_rows < deep + rows, has_down))

    def tall_speed(snap, comp, at, size):
        side = pl.multiple_of(at - vel_start, LANE)
        top = side_speed[0, snap, comp, :, pl.ds(side, size)].astype(f32)[16 - deep :]
        bottom = side_speed[1, snap, comp, :, pl.ds(side, size)].astype(f32)[:deep]
        return jnp.concatenate([top, speed(snap, comp, at, size), bottom], 0)

    def clip_side(at):
        return pl.multiple_of(jnp.clip(base + at, vel_start, vel_start + wide - LANE), LANE)

    wait_sides(speed_sides())
    if chain:
        for block in range(blocks - 1, 1, -1):
            if block < blocks - 1:
                need(block)
            start_sides(slab_sides(block))
        wait_sides(slab_sides(blocks - 1))
    for block, i in chain:
        dst = solved.at[block, i % 2]
        if i == 0:
            if block > 1:
                wait_sides(slab_sides(block))
            else:
                need(block)
        snap = part_snap(block, i)
        for at, size in pieces:
            vel_at = clip_side(at) if size == LANE else piece_vel(at, size)
            new = stencil(
                src, at + LANE, vel_at, clip_side(at - LANE), clip_side(at + size), size,
                snap, COARSE, None, at, tall_speed,
            )
            if i == 0:
                new = new + gathered[block, :, at + LANE : at + LANE + size]
            keep = inside
            if at == 0:
                keep = jnp.logical_and(inside, t > 0)
            if at == LANE + part:
                keep = jnp.logical_and(inside, t < blocks - 1)
            dst[:, at + LANE : at + LANE + size] = jnp.where(keep, new, 0.0)
        if i == 0:
            deliver(block - 1, dst)
            delivered.append((block - 1, dst))
        src = dst

    for sender in range(blocks):

        @pl.when(jnp.logical_and(t < blocks - 1, t != sender))
        def _():
            incoming_copy(t, gathered.at[0], sender).wait_recv()

    ready = set()
    idx_corr = new_edge()

    def start_all(at):
        value = incoming[:, pl.ds(at + LANE, width)]
        put_edges(value, at, width, snap_coarse[points - 1], COARSE, idx_corr, at)
        x_buf[points - 1, 0, :, pl.ds(at + LANE, width)] = value + next_guess[:, pl.ds(at + LANE, width)]
        total[:, pl.ds(at, width)] = jnp.zeros((rows, width), f32)

    over_columns(start_all)
    send_edges(idx_corr, cols)

    def correction_chain():
        src, idx = incoming, idx_corr
        for i in range(points - 1, -1, -1):
            nxt = new_edge() if i > 0 else None
            dst = corr_buf.at[i]
            wait_edges(idx, cols)

            def work(at, src=src, dst=dst, idx=idx, nxt=nxt, i=i):
                new = full_stencil(src, at, snap_coarse[i], COARSE, idx)
                new = new + res_buf[i, :, pl.ds(at + LANE, width)]
                value = guess_ref[i, :, pl.ds(at, width)] + new
                cval_ref[i, :, pl.ds(at, width)] = value
                total[:, pl.ds(at, width)] += value
                if i > 0:
                    dst[:, pl.ds(at + LANE, width)] = new
                    put_edges(new, at, width, snap_coarse[i - 1], COARSE, nxt, at)
                    x_buf[i - 1, 0, :, pl.ds(at + LANE, width)] = value

            over_columns(work)
            if i > 0:
                send_edges(nxt, cols)
                ready.add(i - 1)
            src, idx = dst, nxt
            yield

    def second_chain(c):
        while c < points - 1 and c not in ready:
            yield
        yield from relax_chain(c, lambda: x_buf.at[c, 0], None, False, True)

    run([second_chain(points - 1), correction_chain()] + [second_chain(c) for c in range(points - 2, -1, -1)])

    def total_copy(to, sender):
        return pltpu.make_async_remote_copy(
            total.at[:, pl.ds(pl.multiple_of(to * part, LANE), part)],
            totals_in.at[sender],
            big_send.at[3, to],
            big_recv.at[3, sender],
            device_id={"tm": to},
        )

    for to in range(blocks):

        @pl.when(t != to)
        def _():
            total_copy(to, t).start()

    for idx, span in used:
        up, down = edge_copies(idx, span)

        @pl.when(has_up)
        def _():
            up.wait_send()

        @pl.when(has_down)
        def _():
            down.wait_send()

    @pl.when(t > 0)
    def _():
        guess_copy().wait_send()
        for to in range(blocks):

            @pl.when(t != to)
            def _():
                slab_copy(to, t).wait_send()

    sent_sides(speed_sides())
    if chain:
        for block in range(2, blocks):
            sent_sides(slab_sides(block))
    for block, ref in delivered:

        @pl.when(t != block)
        def _():
            incoming_copy(block, ref, t).wait_send()

    for other in range(blocks):

        @pl.when(t != other)
        def _():
            total_copy(t, other).wait_recv()

    scale = 1.0 / (steps * blocks)
    for at in range(0, part, width):
        own = total[:, pl.ds(pl.multiple_of(t * part + at, LANE), width)]
        for other in range(blocks):
            got = totals_in[other, :, at : at + width]
            own = own + jnp.where(t == other, 0.0, got)
        grad_ref[:, at : at + width] = own * scale
    for to in range(blocks):

        @pl.when(t != to)
        def _():
            total_copy(to, t).wait_send()


def body(blocks, strips, guess, sources, velocity, snapshot):
    points, rows, cols = guess.shape
    steps = sources.shape[0]
    factor = steps // points
    part = cols // blocks
    padded = cols + 2 * LANE
    deep = 8 if points * (blocks - 2) <= 8 else 16
    edges = points * (2 * factor + 1) + 2 * points + points * blocks
    f32 = jnp.float32
    vmem = pl.BlockSpec(memory_space=pltpu.VMEM)
    return pl.pallas_call(
        functools.partial(kernel, blocks, strips),
        out_shape=(
            jax.ShapeDtypeStruct((points, rows, cols), f32),
            jax.ShapeDtypeStruct((rows, part), f32),
        ),
        in_specs=[pl.BlockSpec(memory_space=pltpu.SMEM), vmem, vmem, vmem],
        out_specs=(vmem, vmem),
        scratch_shapes=[
            pltpu.VMEM((points, 2, rows, padded), f32),
            pltpu.VMEM((rows, padded), f32),
            pltpu.VMEM((points, rows, padded), f32),
            pltpu.VMEM((rows, padded), f32),
            pltpu.VMEM((blocks, rows + 2 * deep, part + 4 * LANE), f32),
            pltpu.VMEM((blocks, 2, rows + 2 * deep, part + 4 * LANE), f32),
            pltpu.VMEM((rows, padded), f32),
            pltpu.VMEM((points, rows, padded), f32),
            pltpu.VMEM((rows, cols), f32),
            pltpu.VMEM((blocks, rows, part), f32),
            pltpu.VMEM((edges, 2, 1, cols), f32),
            pltpu.VMEM((edges, 2, 1, cols), f32),
            pltpu.SemaphoreType.DMA((edges, 2)),
            pltpu.SemaphoreType.DMA((edges, 2)),
            pltpu.VMEM((2,) + velocity.shape[:2] + (16, part + 2 * LANE), velocity.dtype),
            pltpu.SemaphoreType.DMA((blocks, 2)),
            pltpu.SemaphoreType.DMA((blocks, 2)),
            pltpu.SemaphoreType.DMA((4, blocks)),
            pltpu.SemaphoreType.DMA((4, blocks)),
        ],
        compiler_params=pltpu.CompilerParams(
            collective_id=0, has_side_effects=True, vmem_limit_bytes=56 * 1024 * 1024
        ),
    )(snapshot, guess, sources, velocity)


def solution(mesh):
    in_specs = (P("tm", "space", None), P("tm", "space", None), P(None, None, "space", None), P())
    out_specs = (P("tm", "space", None), P("space", "tm"))
    fn = functools.partial(body, mesh.shape["tm"], mesh.shape["space"])
    return jax.shard_map(fn, mesh=mesh, in_specs=in_specs, out_specs=out_specs, check_vma=False)
```

```python
import functools

import jax
import jax.numpy as jnp
from jax import lax
from jax.experimental import pallas as pl
from jax.experimental.pallas import tpu as pltpu
from jax.sharding import PartitionSpec as P

FINE = (0.2, 0.15)
COARSE = (0.24, 0.2)
LANE = 128


def kernel(
    blocks,
    strips,
    snap_ref,
    guess_ref,
    src_ref,
    vel_ref,
    cval_ref,
    grad_ref,
    x_buf,
    next_guess,
    res_buf,
    b_buf,
    gathered,
    solved,
    incoming,
    corr_buf,
    total,
    totals_in,
    edge_out,
    edge_in,
    edge_send,
    edge_recv,
    side_speed,
    side_send,
    side_recv,
    big_send,
    big_recv,
):
    points, rows, cols = guess_ref.shape
    steps = src_ref.shape[0]
    factor = steps // points
    part = cols // blocks
    width = min(1024, part)
    deep = (gathered.shape[1] - rows) // 2
    wide = part + 2 * LANE
    t = lax.axis_index("tm")
    s = lax.axis_index("space")
    has_up = s > 0
    has_down = s < strips - 1
    f32 = jnp.float32

    barrier = pltpu.get_barrier_semaphore()
    for d in range(1, blocks):
        pl.semaphore_signal(barrier, 1, device_id={"tm": lax.rem(t + d, blocks)})

    @pl.when(has_up)
    def _():
        pl.semaphore_signal(barrier, 1, device_id={"space": s - 1})

    @pl.when(has_down)
    def _():
        pl.semaphore_signal(barrier, 1, device_id={"space": s + 1})

    def clear_margin(ref, size):
        zero = jnp.zeros((ref.shape[0], LANE), f32)
        ref[:, 0:LANE] = zero
        ref[:, size - LANE : size] = zero

    for c in range(points):
        for slot in range(2):
            clear_margin(x_buf.at[c, slot], cols + 2 * LANE)
        clear_margin(res_buf.at[c], cols + 2 * LANE)
        clear_margin(corr_buf.at[c], cols + 2 * LANE)
    clear_margin(next_guess, cols + 2 * LANE)
    clear_margin(b_buf, cols + 2 * LANE)
    clear_margin(incoming, cols + 2 * LANE)
    for i in range(blocks):
        clear_margin(gathered.at[i], part + 4 * LANE)
        for slot in range(2):
            clear_margin(solved.at[i, slot], part + 4 * LANE)
    rounds = edge_in.shape[0]

    @pl.when(jnp.logical_not(has_up))
    def _():
        def zero_top(i, carry):
            edge_in[i, 0] = jnp.zeros((1, cols), f32)
            return carry

        lax.fori_loop(0, rounds, zero_top, 0)
        side_speed[0] = jnp.zeros(side_speed.shape[1:], side_speed.dtype)
        for block in range(2, blocks):
            gathered[block, 0:deep, LANE : LANE + wide] = jnp.zeros((deep, wide), f32)

    @pl.when(jnp.logical_not(has_down))
    def _():
        def zero_bottom(i, carry):
            edge_in[i, 1] = jnp.zeros((1, cols), f32)
            return carry

        lax.fori_loop(0, rounds, zero_bottom, 0)
        side_speed[1] = jnp.zeros(side_speed.shape[1:], side_speed.dtype)
        for block in range(2, blocks):
            gathered[block, deep + rows : rows + 2 * deep, LANE : LANE + wide] = jnp.zeros((deep, wide), f32)

    def over_columns(fn):
        def step(k, carry):
            fn(pl.multiple_of(k * width, width))
            return carry

        lax.fori_loop(0, cols // width, step, 0)

    @pl.when(t == blocks - 1)
    def _():
        def clear(at):
            next_guess[:, pl.ds(at + LANE, width)] = jnp.zeros((rows, width), f32)
            incoming[:, pl.ds(at + LANE, width)] = jnp.zeros((rows, width), f32)

        over_columns(clear)

    peers = blocks - 1 + jnp.minimum(s, 1) + jnp.minimum(strips - 1 - s, 1)
    pl.semaphore_wait(barrier, peers)

    def edge_copies(idx, at):
        window = pl.ds(at, width)
        k = at // width
        return (
            pltpu.make_async_remote_copy(
                edge_out.at[idx, 0, :, window],
                edge_in.at[idx, 1, :, window],
                edge_send.at[idx, 0, k],
                edge_recv.at[idx, 1, k],
                device_id={"space": s - 1},
            ),
            pltpu.make_async_remote_copy(
                edge_out.at[idx, 1, :, window],
                edge_in.at[idx, 0, :, window],
                edge_send.at[idx, 1, k],
                edge_recv.at[idx, 0, k],
                device_id={"space": s + 1},
            ),
        )

    used = set()

    def send_edges(idx, at):
        used.add(idx)
        up, down = edge_copies(idx, at)

        @pl.when(has_up)
        def _():
            up.start()

        @pl.when(has_down)
        def _():
            down.start()

    def wait_edges(idx, at):
        up, down = edge_copies(idx, at)

        @pl.when(has_up)
        def _():
            down.wait_recv()

        @pl.when(has_down)
        def _():
            up.wait_recv()

    counter = [0]

    def new_edge():
        counter[0] += 1
        return counter[0] - 1

    def speed(snap, comp, at, size):
        return vel_ref[snap, comp, :, pl.ds(at, size)].astype(f32)

    row_no = lax.broadcasted_iota(jnp.int32, (rows, 1), 0)

    def stencil(src, at, vel_at, left_at, right_at, size, snap, kind, idx, edge_at, speed_of=None):
        nu, h = kind
        speed_of = speed_of or speed
        p = src[:, pl.ds(at, size)]
        p_left = src[:, pl.ds(at - LANE, LANE)]
        p_right = src[:, pl.ds(at + size, LANE)]
        hay = h * speed_of(snap, 1, vel_at, size)
        hay_left = h * speed_of(snap, 1, left_at, LANE)
        hay_right = h * speed_of(snap, 1, right_at, LANE)
        hax = h * speed_of(snap, 0, vel_at, size)
        east = jnp.concatenate([(nu + hay) * p, (nu + hay_right) * p_right], 1)
        east = pltpu.roll(east, size + LANE - 1, 1)[:, :size]
        west = jnp.concatenate([(nu - hay_left) * p_left, (nu - hay) * p], 1)
        west = pltpu.roll(west, 1, 1)[:, LANE:]
        below = pltpu.roll((nu + hax) * p, p.shape[0] - 1, 0)
        above = pltpu.roll((nu - hax) * p, 1, 0)
        if idx is not None:
            below = jnp.where(row_no == rows - 1, edge_in[idx, 1, :, pl.ds(edge_at, size)], below)
            above = jnp.where(row_no == 0, edge_in[idx, 0, :, pl.ds(edge_at, size)], above)
        return (1.0 - 4.0 * nu) * p + (east + west) + (below + above)

    def put_edges(value, vel_at, size, snap, kind, idx, edge_at):
        nu, h = kind
        first = vel_ref[snap, 0, 0:16, pl.ds(vel_at, size)].astype(f32)[0:1]
        last = vel_ref[snap, 0, rows - 16 : rows, pl.ds(vel_at, size)].astype(f32)[15:16]
        edge_out[idx, 0, :, pl.ds(edge_at, size)] = (nu + h * first) * value[0:1]
        edge_out[idx, 1, :, pl.ds(edge_at, size)] = (nu - h * last) * value[rows - 1 : rows]
        send_edges(idx, edge_at)

    def snap_at(local):
        return snap_ref[t * steps + local]

    def full_stencil(src, at, snap, kind, idx):
        wait_edges(idx, at)
        left = pl.multiple_of(jnp.maximum(at - LANE, 0), LANE)
        right = pl.multiple_of(jnp.minimum(at + width, cols - LANE), LANE)
        return stencil(src, at + LANE, at, left, right, width, snap, kind, idx, at)

    def guess_copy():
        return pltpu.make_async_remote_copy(
            guess_ref.at[0],
            next_guess.at[:, pl.ds(LANE, cols)],
            big_send.at[0, 0],
            big_recv.at[0, 0],
            device_id={"tm": t - 1},
        )

    @pl.when(t > 0)
    def _():
        guess_copy().start()

    vel_start = pl.multiple_of(jnp.clip(t * part - LANE, 0, cols - wide), LANE)

    def to_sides(up_src, up_dst, down_src, down_dst, number):
        return (
            pltpu.make_async_remote_copy(
                up_src, up_dst, side_send.at[number, 0], side_recv.at[number, 1], device_id={"space": s - 1}
            ),
            pltpu.make_async_remote_copy(
                down_src, down_dst, side_send.at[number, 1], side_recv.at[number, 0], device_id={"space": s + 1}
            ),
        )

    def speed_sides():
        window = pl.ds(vel_start, wide)
        return to_sides(
            vel_ref.at[:, :, 0:16, window],
            side_speed.at[1],
            vel_ref.at[:, :, rows - 16 : rows, window],
            side_speed.at[0],
            0,
        )

    def slab_sides(block):
        window = pl.ds(LANE, wide)
        return to_sides(
            gathered.at[block, deep : 2 * deep, window],
            gathered.at[block, deep + rows : rows + 2 * deep, window],
            gathered.at[block, rows : rows + deep, window],
            gathered.at[block, 0:deep, window],
            block,
        )

    def start_sides(copies):
        up, down = copies

        @pl.when(has_up)
        def _():
            up.start()

        @pl.when(has_down)
        def _():
            down.start()

    def wait_sides(copies):
        up, down = copies

        @pl.when(has_up)
        def _():
            down.wait_recv()

        @pl.when(has_down)
        def _():
            up.wait_recv()

    def sent_sides(copies):
        up, down = copies

        @pl.when(has_up)
        def _():
            up.wait_send()

        @pl.when(has_down)
        def _():
            down.wait_send()

    def relax_chain(c, make_src, finish_last, with_residual, accumulate):
        src = make_src()
        idx = new_edge()
        snap = snap_at(c * factor + factor - 1)

        def first(at):
            put_edges(src[:, pl.ds(at + LANE, width)], at, width, snap, FINE, idx, at)

        over_columns(first)
        yield
        slot = 1
        last = 0 if with_residual else 1
        for offset in range(factor - 1, last - 1, -1):
            n = c * factor + offset
            snap = snap_at(n)
            dst = x_buf.at[c, slot]
            more = offset > last
            nxt = new_edge() if more else None
            snap_next = snap_at(n - 1) if more else None

            def work(at, src=src, dst=dst, idx=idx, nxt=nxt, snap=snap, snap_next=snap_next, n=n, offset=offset, more=more):
                new = full_stencil(src, at, snap, FINE, idx)
                new = new + src_ref[n, :, pl.ds(at, width)].astype(f32)
                if more:
                    put_edges(new, at, width, snap_next, FINE, nxt, at)
                    dst[:, pl.ds(at + LANE, width)] = new
                if accumulate:
                    total[:, pl.ds(at, width)] += new
                if accumulate and not more and c == 0:
                    leave(at)
                if offset == 0:
                    finish_last(at, new)

            over_columns(work)
            src, idx, slot = dst, nxt, 1 - slot
            yield

    lead = 1

    def run(chains):
        chains = list(chains)
        while chains:
            alive = []
            for chain in chains:
                try:
                    next(chain)
                    alive.append(chain)
                except StopIteration:
                    pass
            chains = alive

    first_coarse = new_edge()
    snap_coarse = [snap_at(c * factor) for c in range(points)]

    def first_src(c):
        def make():
            if c < points - 1:

                def fill(at):
                    x_buf[c, 0, :, pl.ds(at + LANE, width)] = guess_ref[c + 1, :, pl.ds(at, width)]

                over_columns(fill)
                return x_buf.at[c, 0]

            @pl.when(t < blocks - 1)
            def _():
                guess_copy().wait_recv()

            return next_guess

        return make

    def first_last(c):
        def finish(at, new):
            value = new - guess_ref[c, :, pl.ds(at, width)]
            res_buf[c, :, pl.ds(at + LANE, width)] = value
            if c == points - 1 and points > 1:
                put_edges(value, at, width, snap_coarse[points - 2], COARSE, first_coarse, at)
            if points == 1:
                b_buf[:, pl.ds(at + LANE, width)] = value

        return finish

    chains = [relax_chain(c, first_src(c), first_last(c), True, False) for c in range(points)]
    for c in range(points - 1):
        for _ in range(lead):
            next(chains[c], None)
    start_sides(speed_sides())
    run(chains)

    src, idx = res_buf.at[points - 1], first_coarse
    for i in range(points - 2, -1, -1):
        nxt = new_edge() if i > 0 else None
        dst = b_buf if i == 0 else x_buf.at[0, i % 2]

        def condense(at, src=src, dst=dst, idx=idx, nxt=nxt, i=i):
            new = full_stencil(src, at, snap_coarse[i], COARSE, idx)
            new = new + res_buf[i, :, pl.ds(at + LANE, width)]
            dst[:, pl.ds(at + LANE, width)] = new
            if i > 0:
                put_edges(new, at, width, snap_coarse[i - 1], COARSE, nxt, at)

        over_columns(condense)
        src, idx = dst, nxt

    def slab_copy(to, sender):
        return pltpu.make_async_remote_copy(
            b_buf.at[:, pl.ds(pl.multiple_of(to * part, LANE), wide)],
            gathered.at[sender, deep : deep + rows, pl.ds(LANE, wide)],
            big_send.at[1, to],
            big_recv.at[1, sender],
            device_id={"tm": to},
        )

    @pl.when(t > 0)
    def _():
        for to in range(blocks):

            @pl.when(t != to)
            def _():
                slab_copy(to, t).start()

        for at in range(0, wide, LANE):
            gathered[t, deep : deep + rows, at + LANE : at + 2 * LANE] = b_buf[
                :, pl.ds(pl.multiple_of(t * part + at, LANE), LANE)
            ]

    def incoming_copy(block, ref, sender):
        return pltpu.make_async_remote_copy(
            ref.at[deep : deep + rows, pl.ds(2 * LANE, part)],
            incoming.at[:, pl.ds(pl.multiple_of(LANE + sender * part, LANE), part)],
            big_send.at[2, block],
            big_recv.at[2, sender],
            device_id={"tm": block},
        )

    piece = min(512, part)
    pieces = [(0, LANE)]
    pieces += [(LANE + k * piece, piece) for k in range(part // piece)]
    pieces += [(LANE + part, LANE)]
    base = t * part - LANE

    def clip(at):
        return pl.multiple_of(jnp.clip(base + at, 0, cols - LANE), LANE)

    def piece_vel(at, size):
        if size == LANE:
            return clip(at)
        return pl.multiple_of(base + at, LANE)

    def need(block):
        @pl.when(t != block)
        def _():
            slab_copy(t, block).wait_recv()

    def deliver(block, ref):
        @pl.when(t != block)
        def _():
            incoming_copy(block, ref, t).start()

        @pl.when(t == block)
        def _():
            for at in range(0, part, LANE):
                incoming[:, pl.ds(pl.multiple_of(LANE + t * part + at, LANE), LANE)] = ref[
                    deep : deep + rows, 2 * LANE + at : 3 * LANE + at
                ]

    need(blocks - 1)
    src = gathered.at[blocks - 1]
    delivered = []
    if blocks > 1:
        deliver(blocks - 2, src)
        delivered.append((blocks - 2, src))
    chain = [(block, i) for block in range(blocks - 2, 0, -1) for i in range(points - 1, -1, -1)]

    def part_snap(block, i):
        return snap_ref[(block * points + i) * factor]

    all_rows = lax.broadcasted_iota(jnp.int32, (rows + 2 * deep, 1), 0)
    inside = jnp.logical_or(all_rows >= deep, has_up)
    inside = jnp.logical_and(inside, jnp.logical_or(all_rows < deep + rows, has_down))

    def tall_speed(snap, comp, at, size):
        side = pl.multiple_of(at - vel_start, LANE)
        top = side_speed[0, snap, comp, :, pl.ds(side, size)].astype(f32)[16 - deep :]
        bottom = side_speed[1, snap, comp, :, pl.ds(side, size)].astype(f32)[:deep]
        return jnp.concatenate([top, speed(snap, comp, at, size), bottom], 0)

    def clip_side(at):
        return pl.multiple_of(jnp.clip(base + at, vel_start, vel_start + wide - LANE), LANE)

    wait_sides(speed_sides())
    if chain:
        for block in range(blocks - 1, 1, -1):
            if block < blocks - 1:
                need(block)
            start_sides(slab_sides(block))
        wait_sides(slab_sides(blocks - 1))
    for block, i in chain:
        dst = solved.at[block, i % 2]
        if i == 0:
            if block > 1:
                wait_sides(slab_sides(block))
            else:
                need(block)
        snap = part_snap(block, i)
        for at, size in pieces:
            vel_at = clip_side(at) if size == LANE else piece_vel(at, size)
            new = stencil(
                src, at + LANE, vel_at, clip_side(at - LANE), clip_side(at + size), size,
                snap, COARSE, None, at, tall_speed,
            )
            if i == 0:
                new = new + gathered[block, :, at + LANE : at + LANE + size]
            keep = inside
            if at == 0:
                keep = jnp.logical_and(inside, t > 0)
            if at == LANE + part:
                keep = jnp.logical_and(inside, t < blocks - 1)
            dst[:, at + LANE : at + LANE + size] = jnp.where(keep, new, 0.0)
        if i == 0:
            deliver(block - 1, dst)
            delivered.append((block - 1, dst))
        src = dst

    def total_copy(to, sender):
        return pltpu.make_async_remote_copy(
            total.at[:, pl.ds(pl.multiple_of(to * part, LANE), part)],
            totals_in.at[sender],
            big_send.at[3, to],
            big_recv.at[3, sender],
            device_id={"tm": to},
        )

    def leave(at):
        if width == part:
            to = at // width

            @pl.when(t != to)
            def _():
                total_copy(to, t).start()

    def arrived(sender):
        @pl.when(jnp.logical_and(t < blocks - 1, t != sender))
        def _():
            incoming_copy(t, gathered.at[0], sender).wait_recv()

    if width != part:
        for sender in range(blocks):
            arrived(sender)

    ready = set()
    idx_corr = new_edge()

    def start_all(at):
        if width == part:
            arrived(at // width)
        value = incoming[:, pl.ds(at + LANE, width)]
        put_edges(value, at, width, snap_coarse[points - 1], COARSE, idx_corr, at)
        x_buf[points - 1, 0, :, pl.ds(at + LANE, width)] = value + next_guess[:, pl.ds(at + LANE, width)]
        total[:, pl.ds(at, width)] = jnp.zeros((rows, width), f32)

    over_columns(start_all)

    def correction_chain():
        src, idx = incoming, idx_corr
        for i in range(points - 1, -1, -1):
            nxt = new_edge() if i > 0 else None
            dst = corr_buf.at[i]

            def work(at, src=src, dst=dst, idx=idx, nxt=nxt, i=i):
                new = full_stencil(src, at, snap_coarse[i], COARSE, idx)
                new = new + res_buf[i, :, pl.ds(at + LANE, width)]
                value = guess_ref[i, :, pl.ds(at, width)] + new
                cval_ref[i, :, pl.ds(at, width)] = value
                total[:, pl.ds(at, width)] += value
                if i > 0:
                    dst[:, pl.ds(at + LANE, width)] = new
                    put_edges(new, at, width, snap_coarse[i - 1], COARSE, nxt, at)
                    x_buf[i - 1, 0, :, pl.ds(at + LANE, width)] = value

            over_columns(work)
            if i > 0:
                ready.add(i - 1)
            src, idx = dst, nxt
            yield

    def second_chain(c):
        while c < points - 1 and c not in ready:
            yield
        yield from relax_chain(c, lambda: x_buf.at[c, 0], None, False, True)

    run([second_chain(points - 1), correction_chain()] + [second_chain(c) for c in range(points - 2, -1, -1)])

    if width != part:
        for to in range(blocks):

            @pl.when(t != to)
            def _():
                total_copy(to, t).start()

    def edges_sent(at):
        for idx in sorted(used):
            up, down = edge_copies(idx, at)

            @pl.when(has_up)
            def _():
                up.wait_send()

            @pl.when(has_down)
            def _():
                down.wait_send()

    over_columns(edges_sent)

    @pl.when(t > 0)
    def _():
        guess_copy().wait_send()
        for to in range(blocks):

            @pl.when(t != to)
            def _():
                slab_copy(to, t).wait_send()

    sent_sides(speed_sides())
    if chain:
        for block in range(2, blocks):
            sent_sides(slab_sides(block))
    for block, ref in delivered:

        @pl.when(t != block)
        def _():
            incoming_copy(block, ref, t).wait_send()

    for other in range(blocks):

        @pl.when(t != other)
        def _():
            total_copy(t, other).wait_recv()

    scale = 1.0 / (steps * blocks)
    for at in range(0, part, width):
        own = total[:, pl.ds(pl.multiple_of(t * part + at, LANE), width)]
        for other in range(blocks):
            got = totals_in[other, :, at : at + width]
            own = own + jnp.where(t == other, 0.0, got)
        grad_ref[:, at : at + width] = own * scale
    for to in range(blocks):

        @pl.when(t != to)
        def _():
            total_copy(to, t).wait_send()


def body(blocks, strips, guess, sources, velocity, snapshot):
    points, rows, cols = guess.shape
    steps = sources.shape[0]
    factor = steps // points
    part = cols // blocks
    padded = cols + 2 * LANE
    deep = 8 if points * (blocks - 2) <= 8 else 16
    edges = points * (2 * factor + 1) + 2 * points + points * blocks
    f32 = jnp.float32
    vmem = pl.BlockSpec(memory_space=pltpu.VMEM)
    return pl.pallas_call(
        functools.partial(kernel, blocks, strips),
        out_shape=(
            jax.ShapeDtypeStruct((points, rows, cols), f32),
            jax.ShapeDtypeStruct((rows, part), f32),
        ),
        in_specs=[pl.BlockSpec(memory_space=pltpu.SMEM), vmem, vmem, vmem],
        out_specs=(vmem, vmem),
        scratch_shapes=[
            pltpu.VMEM((points, 2, rows, padded), f32),
            pltpu.VMEM((rows, padded), f32),
            pltpu.VMEM((points, rows, padded), f32),
            pltpu.VMEM((rows, padded), f32),
            pltpu.VMEM((blocks, rows + 2 * deep, part + 4 * LANE), f32),
            pltpu.VMEM((blocks, 2, rows + 2 * deep, part + 4 * LANE), f32),
            pltpu.VMEM((rows, padded), f32),
            pltpu.VMEM((points, rows, padded), f32),
            pltpu.VMEM((rows, cols), f32),
            pltpu.VMEM((blocks, rows, part), f32),
            pltpu.VMEM((edges, 2, 1, cols), f32),
            pltpu.VMEM((edges, 2, 1, cols), f32),
            pltpu.SemaphoreType.DMA((edges, 2, blocks * max(1, part // 1024))),
            pltpu.SemaphoreType.DMA((edges, 2, blocks * max(1, part // 1024))),
            pltpu.VMEM((2,) + velocity.shape[:2] + (16, part + 2 * LANE), velocity.dtype),
            pltpu.SemaphoreType.DMA((blocks, 2)),
            pltpu.SemaphoreType.DMA((blocks, 2)),
            pltpu.SemaphoreType.DMA((4, blocks)),
            pltpu.SemaphoreType.DMA((4, blocks)),
        ],
        compiler_params=pltpu.CompilerParams(
            collective_id=0, has_side_effects=True, vmem_limit_bytes=56 * 1024 * 1024
        ),
    )(snapshot, guess, sources, velocity)


def solution(mesh):
    in_specs = (P("tm", "space", None), P("tm", "space", None), P(None, None, "space", None), P())
    out_specs = (P("tm", "space", None), P("space", "tm"))
    fn = functools.partial(body, mesh.shape["tm"], mesh.shape["space"])
    return jax.shard_map(fn, mesh=mesh, in_specs=in_specs, out_specs=out_specs, check_vma=False)
```
